256 devices in a mesh: dp: 32 (over x, y, core), tensor: 8 (over z).
Axes of the slice: x: 4, y: 4, z: 8, core: 2. Of those that a mesh axis runs over, the one named last changes fastest.
Arguments:
- tokens: bfloat16 [32, 1024, 8192], P('dp', 'tensor'), may hold values from -6 to 6
- cotangent: bfloat16 [32, 1024, 2048], P('dp', None, 'tensor'), may hold values from -0.1875 to 0.1875
- error_buffer: bfloat16 [32, 8192, 2048], P('dp', None, 'tensor'), may hold values from -4 to 4
- start_basis: float32 [2048, 32], P('tensor'), may hold values from -0.125 to 0.125
Outputs:
- decompressed: bfloat16 [8192, 2048], P('dp', 'tensor')
- new_error: bfloat16 [32, 8192, 2048], P('dp', None, 'tensor')
The draws below stay inside these ranges and needn't reach their ends.
All inputs are finite; a program needn't handle non-finite values.
Results may differ from the reference program's by a relative error of at most 0.00105.
Values may be sent and summed in bfloat16 or wider, within the bound.
No kernel may reach another device: no remote copies, remote signals or barrier semaphores. Data moves between devices by JAX's collectives and lax.ppermute only.
A program may use at most 128 MiB of HBM per device.

```python
import jax
import jax.numpy as jnp
from jax import lax

D = 8192
R = 32
TOK = 1024
COLS = 2048
REPLICAS = 32
N_DP = 32


def levels(stream_key, shape, cuts, least, largest):
    gain, own = 1.0, jax.random.fold_in(stream_key, 6)
    for dim, parts in cuts:
        steps = jnp.exp(jax.random.uniform(jax.random.fold_in(own, dim), (parts,), jnp.float32, least / len(cuts), largest / len(cuts)))
        gain = gain * jnp.repeat(steps, shape[dim] // parts).reshape([-1 if axis == dim else 1 for axis in range(len(shape))])
    return gain


def noise(own_key, shape, scale, reach, cuts=(), dtype=jnp.bfloat16):
    result = jax.random.normal(own_key, shape, jnp.float32) * scale
    if len(cuts) > 0:
        result = levels(own_key, shape, cuts, -0.22, 0.18) * result
    return jnp.clip(result, min=-reach, max=reach).astype(dtype)


def setup_inputs(seed: int = 0) -> dict:
    streams_of = jax.random.split(jax.random.key(seed), 5)
    tokens = noise(streams_of[0], (REPLICAS, TOK, D), 1.0, 6.0, ((0, 32), (1, 8)))
    cotangent = noise(streams_of[1], (REPLICAS, TOK, COLS), TOK ** -0.5, 0.1875, ((0, 32), (2, 8)))
    error_buffer = noise(streams_of[2], (REPLICAS, D, COLS), 0.5, 4.0, ((0, 32), (2, 8)))
    start_basis = noise(streams_of[3], (COLS, R), COLS ** -0.5, 0.125, ((0, 8),), jnp.float32)
    return dict(tokens=tokens, cotangent=cotangent, error_buffer=error_buffer, start_basis=start_basis)


def replica_merged(bundle):
    inputs, cotangent, error_buffer = bundle
    gradient = lax.dot_general(inputs.astype(jnp.float32), cotangent.astype(jnp.float32), (((0,), (0,)), ((), ())), preferred_element_type=jnp.float32)
    return gradient + error_buffer.astype(jnp.float32)

def reference(tokens, cotangent, error_buffer, start_basis):
    highest = lax.Precision.HIGHEST
    merged = lax.map(replica_merged, (tokens, cotangent, error_buffer))
    left_factor = jnp.einsum('rdc,ck->dk', merged, start_basis, precision=highest)
    orthogonal, triangle = jnp.linalg.qr(left_factor)
    basis = orthogonal * jnp.sign(jnp.diagonal(triangle))[None, :]
    right_factor = jnp.einsum('rdc,dk->ck', merged, basis, precision=highest)
    product = jnp.dot(basis, right_factor.T, precision=highest)
    decompressed = product.astype(jnp.bfloat16)
    new_error = (merged - product[None] / N_DP).astype(jnp.bfloat16)
    return (decompressed, new_error)
```

```python
import jax
import jax.numpy as jnp
from jax import lax
from jax.experimental import pallas as pl
from jax.experimental.pallas import tpu as pltpu
from jax.sharding import PartitionSpec as P

F32 = jnp.float32
BF16 = jnp.bfloat16
GATHERED = 8
CHUNKS = 8
DEEP = 2
TIES = (-1, -1, -1, -1, -1, -1)
TILE = 1024
BUFFERS = 2
VMEM = 56 << 20


def split(x):
    high = lax.reduce_precision(x, 8, 7)
    rest = x - high
    middle = lax.reduce_precision(rest, 8, 7)
    return high.astype(BF16), middle.astype(BF16), (rest - middle).astype(BF16)


def split_rows(x):
    return jnp.concatenate(split(x), axis=0)


def join_rows(x):
    rank = x.shape[0] // 3
    return (x[2 * rank :] + x[rank : 2 * rank]) + x[:rank]


def dot(a, b, dims):
    return lax.dot_general(a, b, (dims, ((), ())), preferred_element_type=F32)


def shift(x, axis, by):
    size = lax.axis_size(axis)
    return lax.ppermute(x, axis, [(j, (j + by) % size) for j in range(size)])


def after(x, *others):
    return lax.optimization_barrier((x,) + others)[0] if others else x


def ring(own, axis, deep):
    size = lax.axis_size(axis)
    half = size // 2
    up, down = list(own), list(own)
    blocks = [[piece] + [None] * (size - 1) for piece in own]
    ups, downs = [], []
    for hop in range(1, half + 1):
        for c in range(len(own)):
            if hop < half or c % 2 == 0:
                up[c] = shift(after(up[c], ups[-deep]) if len(ups) >= deep else up[c], axis, 1)
                blocks[c][size - hop] = up[c]
                ups.append(up[c])
            if hop < half or c % 2 == 1:
                down[c] = shift(after(down[c], downs[-deep]) if len(downs) >= deep else down[c], axis, -1)
                blocks[c][hop] = down[c]
                downs.append(down[c])
    return blocks, list(zip(ups, downs))


def finish_kernel(count, *refs):
    blocks, (cot_ref, right_ref, basis_ref, error_ref), out_ref = refs[:count], refs[count : count + 4], refs[-1]
    if count == 1:
        whole = blocks[0][...]
    else:
        whole = jnp.concatenate([block[...] for block in blocks], axis=0)
    total = dot(basis_ref[...], right_ref[...], ((0,), (0,))) + dot(whole, cot_ref[...], ((0,), (0,)))
    out_ref[...] = (total + error_ref[...].astype(F32)).astype(BF16)


def finish(start, blocks, cot, right_wide, basis_wide, error, out):
    count = len(blocks)
    depth, width = blocks[0].shape
    rows, columns = error.shape
    tile = TILE
    inside = cot.shape[0]
    extra = right_wide.shape[0]
    at = lambda i: start // tile + i
    deep = dict(pipeline_mode=pl.Buffered(BUFFERS)) if width // tile > 2 else {}
    in_specs = [pl.BlockSpec((depth, tile), lambda i: (0, i), **deep) for _ in range(count)] + [
        pl.BlockSpec((inside, columns), lambda i: (0, 0)),
        pl.BlockSpec((extra, columns), lambda i: (0, 0)),
        pl.BlockSpec((extra, tile), lambda i: (0, at(i)), **deep),
        pl.BlockSpec((tile, columns), lambda i: (at(i), 0), **deep),
    ]
    operands = list(blocks) + [cot, right_wide, basis_wide, error]
    aliases = {}
    if out is not None:
        in_specs.append(pl.BlockSpec(memory_space=pl.ANY))
        operands.append(out)
        aliases = {len(operands) - 1: 0}
    return pl.pallas_call(
        lambda *refs: finish_kernel(count, *refs),
        grid=(width // tile,),
        in_specs=in_specs,
        out_specs=pl.BlockSpec((tile, columns), lambda i: (at(i), 0)),
        out_shape=jax.ShapeDtypeStruct((rows, columns), BF16),
        input_output_aliases=aliases,
        compiler_params=pltpu.CompilerParams(vmem_limit_bytes=VMEM),
        cost_estimate=pl.CostEstimate(
            flops=2 * inside * width * columns, bytes_accessed=2 * width * (inside + 2 * columns), transcendentals=0
        ),
    )(*operands)


def gather(x, axis):
    return lax.all_to_all(jnp.broadcast_to(x, (lax.axis_size(axis),) + x.shape), axis, 0, 0)


def shards(tokens, cotangent, error_buffer, start_basis):
    highest = lax.Precision.HIGHEST
    tokens, cot, error = tokens[0], cotangent[0], error_buffer[0]
    planes = lax.axis_size("tensor")
    replicas = lax.axis_size("dp")
    depth, d = tokens.shape
    columns, rank = start_basis.shape
    width = d // CHUNKS
    cut = GATHERED * width
    if GATHERED > 0:
        gathered = lax.all_gather(tokens[:, :cut], "tensor", axis=0, tiled=True)
    blocks, events = ring([tokens[:, c * width : (c + 1) * width] for c in range(GATHERED, CHUNKS)], "tensor", DEEP)

    def tie(x, stage):
        return after(x, *events[TIES[stage]]) if TIES[stage] >= 0 else x

    start3 = split_rows(start_basis.T)
    weights = join_rows(dot(start3, cot, ((1,), (1,))))
    weights = weights.reshape(rank, planes, depth).transpose(1, 0, 2)
    weight = tie(jnp.sum(lax.all_to_all(weights, "tensor", 0, 0), axis=0), 0)
    left_part = join_rows(dot(split_rows(weight), tokens, ((1,), (0,))) + dot(start3, error, ((1,), (1,))))
    height = d // replicas
    left_part = left_part.reshape(rank, replicas, height).transpose(1, 0, 2)
    left_rows = jnp.sum(lax.all_to_all(left_part, "dp", 0, 0), axis=0)
    left_rows = tie(left_rows, 1)
    whole_rows = tie(jnp.sum(gather(left_rows, "tensor"), axis=0), 2)
    left = gather(whole_rows, "dp").transpose(1, 0, 2).reshape(rank, d)
    left = tie(left, 3)

    left3 = split_rows(left)
    inner = join_rows(dot(left3, tokens, ((1,), (1,))))
    inner = gather(inner, "tensor").transpose(1, 0, 2).reshape(rank, planes * depth)
    inner = tie(inner, 4)
    right_part = join_rows(dot(split_rows(inner), cot, ((1,), (0,))) + dot(left3, error, ((1,), (0,))))
    right = tie(jnp.sum(gather(right_part, "dp"), axis=0), 5)

    gram = lax.dot_general(left, left, (((1,), (1,)), ((), ())), precision=highest, preferred_element_type=F32)
    triangle = jnp.linalg.cholesky(gram)
    inverse = lax.linalg.triangular_solve(triangle, jnp.eye(rank, dtype=F32), left_side=True, lower=True)
    basis = jnp.dot(inverse, left, precision=highest)
    right = jnp.dot(inverse, right, precision=highest)

    mine = lax.dynamic_slice_in_dim(basis, lax.axis_index("dp") * height, height, 1)
    decompressed = lax.dot_general(
        mine, right, (((0,), (0,)), ((), ())), precision=highest, preferred_element_type=F32
    ).astype(BF16)

    bh, bm, bl = split(basis)
    rh, rm, rl = split(right * (-1.0 / replicas))
    basis_wide = jnp.concatenate([bh, bm, bh, bm, bl, bh], axis=0)
    right_wide = jnp.concatenate([rh, rh, rm, rm, rh, rl], axis=0)
    out = None
    if GATHERED < CHUNKS:
        place = lax.axis_index("tensor") * depth
        turned = lax.dynamic_slice_in_dim(jnp.concatenate([cot, cot], axis=0), place, planes * depth, 0)
        for c, piece in enumerate(blocks):
            out = finish((GATHERED + c) * width, piece, turned, right_wide, basis_wide, error, out)
    if GATHERED > 0:
        out = finish(0, [gathered], cot, right_wide, basis_wide, error, out)
    return decompressed, out[None]


def solution(mesh):
    in_specs = (
        P("dp", "tensor", None),
        P("dp", None, "tensor"),
        P("dp", None, "tensor"),
        P("tensor", None),
    )
    out_specs = (P("dp", "tensor"), P("dp", None, "tensor"))
    return jax.shard_map(shards, mesh=mesh, in_specs=in_specs, out_specs=out_specs, check_vma=False)
```

```python
import jax
import jax.numpy as jnp
from jax import lax
from jax.experimental import pallas as pl
from jax.experimental.pallas import tpu as pltpu
from jax.sharding import PartitionSpec as P

F32 = jnp.float32
BF16 = jnp.bfloat16
CHUNKS = 2
TILE = 1024
LAST = 2048


def split(x):
    high = lax.reduce_precision(x, 8, 7)
    rest = x - high
    middle = lax.reduce_precision(rest, 8, 7)
    return high.astype(BF16), middle.astype(BF16), (rest - middle).astype(BF16)


def split_rows(x):
    return jnp.concatenate(split(x), axis=0)


def join_rows(x):
    rank = x.shape[0] // 3
    return (x[2 * rank :] + x[rank : 2 * rank]) + x[:rank]


def dot(a, b, dims):
    return lax.dot_general(a, b, (dims, ((), ())), preferred_element_type=F32)


def shift(x, axis, by):
    size = lax.axis_size(axis)
    return lax.ppermute(x, axis, [(j, (j + by) % size) for j in range(size)])


def after(x, *others):
    return lax.optimization_barrier((x,) + others)[0] if others else x


class Ring:

    def __init__(self, own, axis):
        self.axis, self.size = axis, lax.axis_size(axis)
        half = self.size // 2
        self.up, self.down = list(own), list(own)
        self.blocks = [[piece] + [None] * (self.size - 1) for piece in own]
        ways = [(hop, c) for hop in range(1, half + 1) for c in range(len(own))]
        self.ups = [(hop, c) for hop, c in ways if hop < half or c % 2 == 0]
        self.downs = [(hop, c) for hop, c in ways if hop < half or c % 2 == 1]

    def step(self, *gate):
        hop, c = self.ups.pop(0)
        self.up[c] = first = shift(after(self.up[c], *gate), self.axis, 1)
        self.blocks[c][self.size - hop] = first
        hop, c = self.downs.pop(0)
        self.down[c] = second = shift(after(self.down[c], *gate), self.axis, -1)
        self.blocks[c][hop] = second
        return first, second


def solve_kernel(left_ref, parts_ref, answer_ref, wide_ref):
    rank = parts_ref.shape[1]
    gram = jnp.zeros((rank, rank), F32)
    for k in (2, 1, 0):
        block = dot(left_ref[...], left_ref[k * rank : (k + 1) * rank, :], ((1,), (1,)))
        gram += join_rows(block)
    row = lax.broadcasted_iota(jnp.int32, (rank, 2 * rank), 0)
    column = lax.broadcasted_iota(jnp.int32, (rank, 2 * rank), 1)
    eye = jnp.where(row + rank == column, 1.0, 0.0).astype(F32)
    both = jnp.concatenate([gram, eye[:, rank:]], axis=1)
    for j in range(rank):
        spread_column = jnp.broadcast_to(both[:, j : j + 1], both.shape)
        scaled = both[j : j + 1, :] / spread_column[j : j + 1, :]
        both = both - jnp.where(row > j, spread_column, 0.0) * scaled
    pivots = jnp.sum(jnp.where(row == column, both, 0.0), axis=1, keepdims=True)
    inverse = both[:, rank:] * (1.0 / jnp.sqrt(pivots))
    total = jnp.sum(parts_ref[...], axis=0)
    exact = dict(precision=lax.Precision.HIGHEST, preferred_element_type=F32)
    right = lax.dot_general(inverse, total, (((1,), (0,)), ((), ())), **exact)
    answer = lax.dot_general(inverse.T, right, (((1,), (0,)), ((), ())), **exact)
    answer_ref[...] = answer
    share = answer * (-1.0 / parts_ref.shape[0])
    high = share.astype(BF16)
    rest = share - high.astype(F32)
    middle = rest.astype(BF16)
    low = (rest - middle.astype(F32)).astype(BF16)
    wide_ref[...] = jnp.concatenate([high, high, middle, middle, high, low], axis=0)


def solve(left3, parts):
    _, rank, columns = parts.shape
    return pl.pallas_call(
        solve_kernel,
        out_shape=(
            jax.ShapeDtypeStruct((rank, columns), F32),
            jax.ShapeDtypeStruct((6 * rank, columns), BF16),
        ),
        compiler_params=pltpu.CompilerParams(vmem_limit_bytes=24 << 20),
        cost_estimate=pl.CostEstimate(flops=1 << 24, bytes_accessed=3 << 20, transcendentals=0),
    )(left3, parts)


def partial_kernel(count, *refs):
    blocks, (cot_ref, right_ref, left_ref, error_ref), out_ref = refs[:count], refs[count : count + 4], refs[-1]
    rank = left_ref.shape[0] // 3
    high, middle, low = (left_ref[k * rank : (k + 1) * rank, :] for k in range(3))
    left = jnp.concatenate([high, middle, high, middle, low, high], axis=0)
    whole = jnp.concatenate([block[...] for block in blocks], axis=0)
    total = dot(left, right_ref[...], ((0,), (0,))) + dot(whole, cot_ref[...], ((0,), (0,)))
    out_ref[...] = total + error_ref[...].astype(F32)


def partial(start, blocks, cot, right_wide, left3, error):
    count = len(blocks)
    depth, width = blocks[0].shape
    columns = error.shape[1]
    inside, extra = cot.shape[0], right_wide.shape[0]
    at = lambda i: start // TILE + i
    return pl.pallas_call(
        lambda *refs: partial_kernel(count, *refs),
        grid=(width // TILE,),
        in_specs=[pl.BlockSpec((depth, TILE), lambda i: (0, i)) for _ in range(count)]
        + [
            pl.BlockSpec((inside, columns), lambda i: (0, 0)),
            pl.BlockSpec((extra, columns), lambda i: (0, 0)),
            pl.BlockSpec((extra // 2, TILE), lambda i: (0, at(i))),
            pl.BlockSpec((TILE, columns), lambda i: (at(i), 0)),
        ],
        out_specs=pl.BlockSpec((TILE, columns), lambda i: (i, 0)),
        out_shape=jax.ShapeDtypeStruct((width, columns), F32),
        compiler_params=pltpu.CompilerParams(vmem_limit_bytes=24 << 20),
        cost_estimate=pl.CostEstimate(
            flops=2 * inside * width * columns, bytes_accessed=2 * width * (inside + 3 * columns), transcendentals=0
        ),
    )(*blocks, cot, right_wide, left3, error)


def finish_kernel(steps, first_ref, second_ref, one_ref, two_ref, cot_ref, out_ref):
    step = pl.program_id(0)

    @pl.when(step < steps)
    def _():
        out_ref[...] = (one_ref[...] + dot(first_ref[...], cot_ref[...], ((0,), (0,)))).astype(BF16)

    @pl.when(step >= steps)
    def _():
        out_ref[...] = (two_ref[...] + dot(second_ref[...], cot_ref[...], ((0,), (0,)))).astype(BF16)


def finish(first, second, one, two, cot):
    depth, width = first.shape
    columns = cot.shape[1]
    steps = width // LAST
    low = lambda i: jnp.minimum(i, steps - 1)
    high = lambda i: jnp.maximum(i - steps, 0)
    return pl.pallas_call(
        lambda *refs: finish_kernel(steps, *refs),
        grid=(2 * steps,),
        in_specs=[
            pl.BlockSpec((depth, LAST), lambda i: (0, low(i))),
            pl.BlockSpec((depth, LAST), lambda i: (0, high(i))),
            pl.BlockSpec((LAST, columns), lambda i: (low(i), 0)),
            pl.BlockSpec((LAST, columns), lambda i: (high(i), 0)),
            pl.BlockSpec((depth, columns), lambda i: (0, 0)),
        ],
        out_specs=pl.BlockSpec((LAST, columns), lambda i: (i, 0)),
        out_shape=jax.ShapeDtypeStruct((2 * width, columns), BF16),
        compiler_params=pltpu.CompilerParams(vmem_limit_bytes=24 << 20),
        cost_estimate=pl.CostEstimate(
            flops=4 * depth * width * columns, bytes_accessed=4 * width * (depth + 3 * columns), transcendentals=0
        ),
    )(first, second, one, two, cot)


def spread(x, axis):
    return jnp.broadcast_to(x, (lax.axis_size(axis),) + x.shape)


def shards(tokens, cotangent, error_buffer, start_basis):
    highest = lax.Precision.HIGHEST
    tokens, cot, error = tokens[0], cotangent[0], error_buffer[0]
    planes = lax.axis_size("tensor")
    replicas = lax.axis_size("dp")
    depth, d = tokens.shape
    columns, rank = start_basis.shape
    width = d // CHUNKS
    ring = Ring([tokens[:, c * width : (c + 1) * width] for c in range(CHUNKS)], "tensor")

    start3 = split_rows(after(start_basis, *ring.up).T)
    weights = join_rows(dot(start3, cot, ((1,), (1,))))
    weights = weights.reshape(rank, planes, depth).transpose(1, 0, 2)
    moved = [ring.step(weights)]
    moved.append(ring.step(weights))
    weight = jnp.sum(lax.all_to_all(weights, "tensor", 0, 0), axis=0)
    left_part = join_rows(dot(split_rows(weight), tokens, ((1,), (0,))) + dot(start3, error, ((1,), (1,))))
    height = d // replicas
    left_part = left_part.reshape(rank, replicas, height).transpose(1, 0, 2)
    left_rows = after(jnp.sum(lax.all_to_all(left_part, "dp", 0, 0), axis=0), *moved[0])
    left_rows = spread(left_rows, "tensor")
    moved.append(ring.step(left_rows))
    moved.append(ring.step(left_rows))
    whole_rows = after(jnp.sum(lax.all_to_all(left_rows, "tensor", 0, 0), axis=0), *moved[1])
    left = lax.all_to_all(spread(whole_rows, "dp"), "dp", 0, 0)
    left = after(left.transpose(1, 0, 2).reshape(rank, d), *moved[2])

    left3 = split_rows(left)
    inner = spread(join_rows(dot(left3, tokens, ((1,), (1,)))), "tensor")
    moved.append(ring.step(inner))
    moved.append(ring.step(inner))
    moved.append(ring.step(inner))
    inner = lax.all_to_all(inner, "tensor", 0, 0).transpose(1, 0, 2).reshape(rank, planes * depth)
    inner = after(inner, *moved[3])
    right_part = join_rows(dot(split_rows(inner), cot, ((1,), (0,))) + dot(left3, error, ((1,), (0,))))
    right_part = spread(right_part, "dp")
    parts = after(lax.all_to_all(right_part, "dp", 0, 0), *moved[4])
    answer, right_wide = solve(left3, parts)
    blocks = ring.blocks

    mine = lax.dynamic_slice_in_dim(left, lax.axis_index("dp") * height, height, 1)
    decompressed = lax.dot_general(
        mine, answer, (((0,), (0,)), ((), ())), precision=highest, preferred_element_type=F32
    ).astype(BF16)

    half = planes // 2
    place = lax.axis_index("tensor") * depth
    turned = lax.dynamic_slice_in_dim(jnp.concatenate([cot, cot], axis=0), place, planes * depth, 0)
    early = jnp.concatenate([turned[: half * depth], turned[(half + 1) * depth :]], axis=0)
    parts = [
        partial(c * width, blocks[c][:half] + blocks[c][half + 1 :], early, right_wide, left3, error)
        for c in range(CHUNKS)
    ]
    out = finish(blocks[0][half], blocks[1][half], *parts, turned[half * depth : (half + 1) * depth])
    return decompressed, out[None]


def solution(mesh):
    in_specs = (
        P("dp", "tensor", None),
        P("dp", None, "tensor"),
        P("dp", None, "tensor"),
        P("tensor", None),
    )
    out_specs = (P("dp", "tensor"), P("dp", None, "tensor"))
    return jax.shard_map(shards, mesh=mesh, in_specs=in_specs, out_specs=out_specs, check_vma=False)
```

```python
import jax
import jax.numpy as jnp
from jax import lax
from jax.experimental import pallas as pl
from jax.experimental.pallas import tpu as pltpu
from jax.sharding import PartitionSpec as P

F32 = jnp.float32
BF16 = jnp.bfloat16
CHUNKS = 2
TILE = 1024
LAST = 2048


def split(x):
    high = lax.reduce_precision(x, 8, 7)
    rest = x - high
    middle = lax.reduce_precision(rest, 8, 7)
    return high.astype(BF16), middle.astype(BF16), (rest - middle).astype(BF16)


def split_rows(x):
    return jnp.concatenate(split(x), axis=0)


def join_rows(x):
    rank = x.shape[0] // 3
    return (x[2 * rank :] + x[rank : 2 * rank]) + x[:rank]


def dot(a, b, dims):
    return lax.dot_general(a, b, (dims, ((), ())), preferred_element_type=F32)


def shift(x, axis, by):
    size = lax.axis_size(axis)
    return lax.ppermute(x, axis, [(j, (j + by) % size) for j in range(size)])


def after(x, *others):
    return lax.optimization_barrier((x,) + others)[0] if others else x


class Ring:

    def __init__(self, own, axis):
        self.axis, self.size = axis, lax.axis_size(axis)
        half = self.size // 2
        self.up, self.down = list(own), list(own)
        self.blocks = [[piece] + [None] * (self.size - 1) for piece in own]
        ways = [(hop, c) for hop in range(1, half + 1) for c in range(len(own))]
        self.ups = [(hop, c) for hop, c in ways if hop < half or c % 2 == 0]
        self.downs = [(hop, c) for hop, c in ways if hop < half or c % 2 == 1]

    def step(self, *gate):
        hop, c = self.ups.pop(0)
        self.up[c] = first = shift(after(self.up[c], *gate), self.axis, 1)
        self.blocks[c][self.size - hop] = first
        hop, c = self.downs.pop(0)
        self.down[c] = second = shift(after(self.down[c], *gate), self.axis, -1)
        self.blocks[c][hop] = second
        return first, second


def factor_kernel(left_ref, inverse_ref):
    rank = inverse_ref.shape[0]
    gram = jnp.zeros((rank, rank), F32)
    for k in (2, 1, 0):
        block = dot(left_ref[...], left_ref[k * rank : (k + 1) * rank, :], ((1,), (1,)))
        gram += join_rows(block)
    row = lax.broadcasted_iota(jnp.int32, (rank, 2 * rank), 0)
    column = lax.broadcasted_iota(jnp.int32, (rank, 2 * rank), 1)
    eye = jnp.where(row + rank == column, 1.0, 0.0).astype(F32)
    both = jnp.concatenate([gram, eye[:, rank:]], axis=1)
    for j in range(rank):
        spread_column = jnp.broadcast_to(both[:, j : j + 1], both.shape)
        scaled = both[j : j + 1, :] / spread_column[j : j + 1, :]
        both = both - jnp.where(row > j, spread_column, 0.0) * scaled
    pivots = jnp.sum(jnp.where(row == column, both, 0.0), axis=1, keepdims=True)
    inverse_ref[...] = both[:, rank:] * (1.0 / jnp.sqrt(pivots))


def factor(left3):
    rank = left3.shape[0] // 3
    return pl.pallas_call(
        factor_kernel,
        out_shape=jax.ShapeDtypeStruct((rank, rank), F32),
        compiler_params=pltpu.CompilerParams(vmem_limit_bytes=8 << 20),
        cost_estimate=pl.CostEstimate(flops=1 << 24, bytes_accessed=3 << 20, transcendentals=0),
    )(left3)


def solve_kernel(inverse_ref, parts_ref, mine_ref, product_ref, wide_ref):
    exact = dict(precision=lax.Precision.HIGHEST, preferred_element_type=F32)
    inverse = inverse_ref[...]
    total = jnp.sum(parts_ref[...], axis=0)
    right = lax.dot_general(inverse, total, (((1,), (0,)), ((), ())), **exact)
    answer = lax.dot_general(inverse.T, right, (((1,), (0,)), ((), ())), **exact)
    product_ref[...] = lax.dot_general(mine_ref[...].T, answer, (((1,), (0,)), ((), ())), **exact).astype(BF16)
    share = answer * (-1.0 / parts_ref.shape[0])
    high = share.astype(BF16)
    rest = share - high.astype(F32)
    middle = rest.astype(BF16)
    low = (rest - middle.astype(F32)).astype(BF16)
    wide_ref[...] = jnp.concatenate([high, high, middle, middle, high, low], axis=0)


def solve(inverse, parts, mine):
    _, rank, columns = parts.shape
    return pl.pallas_call(
        solve_kernel,
        out_shape=(
            jax.ShapeDtypeStruct((mine.shape[1], columns), BF16),
            jax.ShapeDtypeStruct((6 * rank, columns), BF16),
        ),
        compiler_params=pltpu.CompilerParams(vmem_limit_bytes=8 << 20),
        cost_estimate=pl.CostEstimate(flops=1 << 24, bytes_accessed=1 << 20, transcendentals=0),
    )(inverse, parts, mine)


def partial_kernel(count, *refs):
    blocks, (cot_ref, right_ref, left_ref, error_ref), out_ref = refs[:count], refs[count : count + 4], refs[-1]
    rank = left_ref.shape[0] // 3
    high, middle, low = (left_ref[k * rank : (k + 1) * rank, :] for k in range(3))
    left = jnp.concatenate([high, middle, high, middle, low, high], axis=0)
    whole = jnp.concatenate([block[...] for block in blocks], axis=0)
    total = dot(left, right_ref[...], ((0,), (0,))) + dot(whole, cot_ref[...], ((0,), (0,)))
    out_ref[...] = total + error_ref[...].astype(F32)


def partial(start, blocks, cot, right_wide, left3, error):
    count = len(blocks)
    depth, width = blocks[0].shape
    columns = error.shape[1]
    inside, extra = cot.shape[0], right_wide.shape[0]
    at = lambda i: start // TILE + i
    return pl.pallas_call(
        lambda *refs: partial_kernel(count, *refs),
        grid=(width // TILE,),
        in_specs=[pl.BlockSpec((depth, TILE), lambda i: (0, i)) for _ in range(count)]
        + [
            pl.BlockSpec((inside, columns), lambda i: (0, 0)),
            pl.BlockSpec((extra, columns), lambda i: (0, 0)),
            pl.BlockSpec((extra // 2, TILE), lambda i: (0, at(i))),
            pl.BlockSpec((TILE, columns), lambda i: (at(i), 0)),
        ],
        out_specs=pl.BlockSpec((TILE, columns), lambda i: (i, 0)),
        out_shape=jax.ShapeDtypeStruct((width, columns), F32),
        compiler_params=pltpu.CompilerParams(vmem_limit_bytes=24 << 20),
        cost_estimate=pl.CostEstimate(
            flops=2 * inside * width * columns, bytes_accessed=2 * width * (inside + 3 * columns), transcendentals=0
        ),
    )(*blocks, cot, right_wide, left3, error)


def early_kernel(count, *refs):
    blocks, (cot_ref, error_ref), out_ref = refs[:count], refs[count : count + 2], refs[-1]
    whole = jnp.concatenate([block[...] for block in blocks], axis=0)
    out_ref[...] = dot(whole, cot_ref[...], ((0,), (0,))) + error_ref[...].astype(F32)


def early_partial(start, blocks, cot, error):
    count = len(blocks)
    depth, width = blocks[0].shape
    inside, columns = cot.shape
    return pl.pallas_call(
        lambda *refs: early_kernel(count, *refs),
        grid=(width // TILE,),
        in_specs=[pl.BlockSpec((depth, TILE), lambda i: (0, i)) for _ in range(count)]
        + [
            pl.BlockSpec((inside, columns), lambda i: (0, 0)),
            pl.BlockSpec((TILE, columns), lambda i: (start // TILE + i, 0)),
        ],
        out_specs=pl.BlockSpec((TILE, columns), lambda i: (i, 0)),
        out_shape=jax.ShapeDtypeStruct((width, columns), F32),
        compiler_params=pltpu.CompilerParams(vmem_limit_bytes=48 << 20),
        cost_estimate=pl.CostEstimate(flops=1 << 20, bytes_accessed=1 << 16, transcendentals=0),
    )(*blocks, cot, error)


def finish_kernel(steps, first_ref, second_ref, one_ref, two_ref, left_ref, right_ref, cot_ref, out_ref):
    step = pl.program_id(0)

    @pl.when(step < steps)
    def _():
        rank = left_ref.shape[0] // 3
        high, middle, low = (left_ref[k * rank : (k + 1) * rank, :] for k in range(3))
        left = jnp.concatenate([high, middle, high, middle, low, high], axis=0)
        product = dot(left, right_ref[...], ((0,), (0,)))
        out_ref[...] = (one_ref[...] + dot(first_ref[...], cot_ref[...], ((0,), (0,))) + product).astype(BF16)

    @pl.when(step >= steps)
    def _():
        out_ref[...] = (two_ref[...] + dot(second_ref[...], cot_ref[...], ((0,), (0,)))).astype(BF16)


def finish(first, second, one, two, left3, right_wide, cot):
    depth, width = first.shape
    columns = cot.shape[1]
    steps = width // LAST
    low = lambda i: jnp.minimum(i, steps - 1)
    high = lambda i: jnp.maximum(i - steps, 0)
    return pl.pallas_call(
        lambda *refs: finish_kernel(steps, *refs),
        grid=(2 * steps,),
        in_specs=[
            pl.BlockSpec((depth, LAST), lambda i: (0, low(i))),
            pl.BlockSpec((depth, LAST), lambda i: (0, high(i))),
            pl.BlockSpec((LAST, columns), lambda i: (low(i), 0)),
            pl.BlockSpec((LAST, columns), lambda i: (high(i), 0)),
            pl.BlockSpec((left3.shape[0], LAST), lambda i: (0, low(i))),
            pl.BlockSpec(right_wide.shape, lambda i: (0, 0)),
            pl.BlockSpec((depth, columns), lambda i: (0, 0)),
        ],
        out_specs=pl.BlockSpec((LAST, columns), lambda i: (i, 0)),
        out_shape=jax.ShapeDtypeStruct((2 * width, columns), BF16),
        compiler_params=pltpu.CompilerParams(vmem_limit_bytes=24 << 20),
        cost_estimate=pl.CostEstimate(
            flops=4 * depth * width * columns, bytes_accessed=4 * width * (depth + 3 * columns), transcendentals=0
        ),
    )(first, second, one, two, left3, right_wide, cot)


def spread(x, axis):
    return jnp.broadcast_to(x, (lax.axis_size(axis),) + x.shape)


def shards(tokens, cotangent, error_buffer, start_basis):
    tokens, cot, error = tokens[0], cotangent[0], error_buffer[0]
    planes = lax.axis_size("tensor")
    replicas = lax.axis_size("dp")
    depth, d = tokens.shape
    columns, rank = start_basis.shape
    width = d // CHUNKS
    ring = Ring([tokens[:, c * width : (c + 1) * width] for c in range(CHUNKS)], "tensor")

    start3 = split_rows(start_basis.T)
    weights = join_rows(dot(start3, cot, ((1,), (1,))))
    weights = weights.reshape(rank, planes, depth).transpose(1, 0, 2)
    moved = [ring.step()]
    moved.append(ring.step(weights))
    weight = after(jnp.sum(lax.all_to_all(weights, "tensor", 0, 0), axis=0), *moved[0])
    moved.append(ring.step(weight))
    left_part = join_rows(dot(split_rows(weight), tokens, ((1,), (0,))) + dot(start3, error, ((1,), (1,))))
    height = d // replicas
    left_part = left_part.reshape(rank, replicas, height).transpose(1, 0, 2)
    left_rows = after(jnp.sum(lax.all_to_all(left_part, "dp", 0, 0), axis=0), *moved[1])
    left_rows = spread(left_rows, "tensor")
    moved.append(ring.step(left_rows))
    whole_rows = after(jnp.sum(lax.all_to_all(left_rows, "tensor", 0, 0), axis=0), *moved[2])
    moved.append(ring.step(whole_rows))
    half = planes // 2
    place = lax.axis_index("tensor") * depth
    turned = lax.dynamic_slice_in_dim(jnp.concatenate([cot, cot], axis=0), place, planes * depth, 0)
    early = jnp.concatenate([turned[: half * depth], turned[(half + 1) * depth :]], axis=0)
    cot_last = turned[half * depth : (half + 1) * depth]
    left = lax.all_to_all(spread(whole_rows, "dp"), "dp", 0, 0)
    left = after(left.transpose(1, 0, 2).reshape(rank, d), early, cot_last, *moved[3])

    left3 = split_rows(left)
    mine = lax.dynamic_slice_in_dim(left, lax.axis_index("dp") * height, height, 1)
    inner = spread(join_rows(dot(left3, tokens, ((1,), (1,)))), "tensor")
    moved.append(ring.step(inner))
    inverse = factor(after(left3, inner))
    inner = lax.all_to_all(inner, "tensor", 0, 0).transpose(1, 0, 2).reshape(rank, planes * depth)
    inner = after(inner, inverse, mine, *moved[4])
    right_part = join_rows(dot(split_rows(inner), cot, ((1,), (0,))) + dot(left3, error, ((1,), (0,))))
    right_part = spread(right_part, "dp")
    moved.append(ring.step(right_part))
    blocks = ring.blocks
    one = early_partial(0, blocks[0][:half] + blocks[0][half + 1 :], early, error)
    parts = after(lax.all_to_all(right_part, "dp", 0, 0), one, *moved[5])
    decompressed, right_wide = solve(inverse, parts, mine)

    two = partial(width, blocks[1][:half] + blocks[1][half + 1 :], early, right_wide, left3, error)
    out = finish(blocks[0][half], blocks[1][half], one, two, left3, right_wide, cot_last)
    return decompressed, out[None]


def solution(mesh):
    in_specs = (
        P("dp", "tensor", None),
        P("dp", None, "tensor"),
        P("dp", None, "tensor"),
        P("tensor", None),
    )
    out_specs = (P("dp", "tensor"), P("dp", None, "tensor"))
    return jax.shard_map(shards, mesh=mesh, in_specs=in_specs, out_specs=out_specs, check_vma=False)
```

```python
import jax
import jax.numpy as jnp
from jax import lax
from jax.experimental import pallas as pl
from jax.experimental.pallas import tpu as pltpu
from jax.sharding import PartitionSpec as P

F32 = jnp.float32
BF16 = jnp.bfloat16
CHUNKS = 2
TILE = 1024
LAST = 2048


def split(x):
    high = lax.reduce_precision(x, 8, 7)
    rest = x - high
    middle = lax.reduce_precision(rest, 8, 7)
    return high.astype(BF16), middle.astype(BF16), (rest - middle).astype(BF16)


def split_rows(x):
    return jnp.concatenate(split(x), axis=0)


def join_rows(x):
    rank = x.shape[0] // 3
    return (x[2 * rank :] + x[rank : 2 * rank]) + x[:rank]


def dot(a, b, dims):
    return lax.dot_general(a, b, (dims, ((), ())), preferred_element_type=F32)


def shift(x, axis, by):
    size = lax.axis_size(axis)
    return lax.ppermute(x, axis, [(j, (j + by) % size) for j in range(size)])


def after(x, *others):
    return lax.optimization_barrier((x,) + others)[0] if others else x


class Ring:

    def __init__(self, own, axis):
        self.axis, self.size = axis, lax.axis_size(axis)
        half = self.size // 2
        self.up, self.down = list(own), list(own)
        self.blocks = [[piece] + [None] * (self.size - 1) for piece in own]
        ways = [(hop, c) for hop in range(1, half + 1) for c in range(len(own))]
        self.ups = [(hop, c) for hop, c in ways if hop < half or c % 2 == 0]
        self.downs = [(hop, c) for hop, c in ways if hop < half or c % 2 == 1]

    def step(self, *gate):
        hop, c = self.ups.pop(0)
        self.up[c] = first = shift(after(self.up[c], *gate), self.axis, 1)
        self.blocks[c][self.size - hop] = first
        hop, c = self.downs.pop(0)
        self.down[c] = second = shift(after(self.down[c], *gate), self.axis, -1)
        self.blocks[c][hop] = second
        return first, second

    def last(self, *gate):
        pieces = []
        for up, down in zip(self.up, self.down):
            pieces.append(shift(after(up[:, :LAST], *gate), self.axis, 1))
            pieces.append(shift(after(down[:, LAST:], *gate), self.axis, -1))
        return pieces


def factor_kernel(left_ref, inverse_ref):
    rank = inverse_ref.shape[0]
    gram = jnp.zeros((rank, rank), F32)
    for k in (2, 1, 0):
        block = dot(left_ref[...], left_ref[k * rank : (k + 1) * rank, :], ((1,), (1,)))
        gram += join_rows(block)
    row = lax.broadcasted_iota(jnp.int32, (rank, 2 * rank), 0)
    column = lax.broadcasted_iota(jnp.int32, (rank, 2 * rank), 1)
    eye = jnp.where(row + rank == column, 1.0, 0.0).astype(F32)
    both = jnp.concatenate([gram, eye[:, rank:]], axis=1)
    for j in range(rank):
        spread_column = jnp.broadcast_to(both[:, j : j + 1], both.shape)
        scaled = both[j : j + 1, :] / spread_column[j : j + 1, :]
        both = both - jnp.where(row > j, spread_column, 0.0) * scaled
    pivots = jnp.sum(jnp.where(row == column, both, 0.0), axis=1, keepdims=True)
    inverse_ref[...] = both[:, rank:] * (1.0 / jnp.sqrt(pivots))


def factor(left3):
    rank = left3.shape[0] // 3
    return pl.pallas_call(
        factor_kernel,
        out_shape=jax.ShapeDtypeStruct((rank, rank), F32),
        compiler_params=pltpu.CompilerParams(vmem_limit_bytes=8 << 20),
        cost_estimate=pl.CostEstimate(flops=1 << 24, bytes_accessed=3 << 20, transcendentals=0),
    )(left3)


def solve_kernel(inverse_ref, parts_ref, mine_ref, product_ref, wide_ref):
    exact = dict(precision=lax.Precision.HIGHEST, preferred_element_type=F32)
    inverse = inverse_ref[...]
    total = jnp.sum(parts_ref[...], axis=0)
    right = lax.dot_general(inverse, total, (((1,), (0,)), ((), ())), **exact)
    answer = lax.dot_general(inverse.T, right, (((1,), (0,)), ((), ())), **exact)
    product_ref[...] = lax.dot_general(mine_ref[...].T, answer, (((1,), (0,)), ((), ())), **exact).astype(BF16)
    share = answer * (-1.0 / parts_ref.shape[0])
    high = share.astype(BF16)
    rest = share - high.astype(F32)
    middle = rest.astype(BF16)
    low = (rest - middle.astype(F32)).astype(BF16)
    wide_ref[...] = jnp.concatenate([high, high, middle, middle, high, low], axis=0)


def solve(inverse, parts, mine):
    _, rank, columns = parts.shape
    return pl.pallas_call(
        solve_kernel,
        out_shape=(
            jax.ShapeDtypeStruct((mine.shape[1], columns), BF16),
            jax.ShapeDtypeStruct((6 * rank, columns), BF16),
        ),
        compiler_params=pltpu.CompilerParams(vmem_limit_bytes=8 << 20),
        cost_estimate=pl.CostEstimate(flops=1 << 24, bytes_accessed=1 << 20, transcendentals=0),
    )(inverse, parts, mine)


def partial_kernel(count, *refs):
    blocks, (cot_ref, right_ref, left_ref, error_ref), out_ref = refs[:count], refs[count : count + 4], refs[-1]
    rank = left_ref.shape[0] // 3
    high, middle, low = (left_ref[k * rank : (k + 1) * rank, :] for k in range(3))
    left = jnp.concatenate([high, middle, high, middle, low, high], axis=0)
    whole = jnp.concatenate([block[...] for block in blocks], axis=0)
    total = dot(left, right_ref[...], ((0,), (0,))) + dot(whole, cot_ref[...], ((0,), (0,)))
    out_ref[...] = total + error_ref[...].astype(F32)


def partial(start, blocks, cot, right_wide, left3, error):
    count = len(blocks)
    depth, width = blocks[0].shape
    columns = error.shape[1]
    inside, extra = cot.shape[0], right_wide.shape[0]
    at = lambda i: start // TILE + i
    return pl.pallas_call(
        lambda *refs: partial_kernel(count, *refs),
        grid=(width // TILE,),
        in_specs=[pl.BlockSpec((depth, TILE), lambda i: (0, i)) for _ in range(count)]
        + [
            pl.BlockSpec((inside, columns), lambda i: (0, 0)),
            pl.BlockSpec((extra, columns), lambda i: (0, 0)),
            pl.BlockSpec((extra // 2, TILE), lambda i: (0, at(i))),
            pl.BlockSpec((TILE, columns), lambda i: (at(i), 0)),
        ],
        out_specs=pl.BlockSpec((TILE, columns), lambda i: (i, 0)),
        out_shape=jax.ShapeDtypeStruct((width, columns), F32),
        compiler_params=pltpu.CompilerParams(vmem_limit_bytes=24 << 20),
        cost_estimate=pl.CostEstimate(
            flops=2 * inside * width * columns, bytes_accessed=2 * width * (inside + 3 * columns), transcendentals=0
        ),
    )(*blocks, cot, right_wide, left3, error)


def early_kernel(count, *refs):
    blocks, (cot_ref, error_ref), out_ref = refs[:count], refs[count : count + 2], refs[-1]
    whole = jnp.concatenate([block[...] for block in blocks], axis=0)
    out_ref[...] = dot(whole, cot_ref[...], ((0,), (0,))) + error_ref[...].astype(F32)


def early_partial(start, blocks, cot, error):
    count = len(blocks)
    depth, width = blocks[0].shape
    inside, columns = cot.shape
    return pl.pallas_call(
        lambda *refs: early_kernel(count, *refs),
        grid=(width // TILE,),
        in_specs=[pl.BlockSpec((depth, TILE), lambda i: (0, i)) for _ in range(count)]
        + [
            pl.BlockSpec((inside, columns), lambda i: (0, 0)),
            pl.BlockSpec((TILE, columns), lambda i: (start // TILE + i, 0)),
        ],
        out_specs=pl.BlockSpec((TILE, columns), lambda i: (i, 0)),
        out_shape=jax.ShapeDtypeStruct((width, columns), F32),
        compiler_params=pltpu.CompilerParams(vmem_limit_bytes=48 << 20),
        cost_estimate=pl.CostEstimate(flops=1 << 20, bytes_accessed=1 << 16, transcendentals=0),
    )(*blocks, cot, error)


def finish_kernel(steps, a_ref, b_ref, c_ref, d_ref, one_ref, two_ref, left_ref, right_ref, cot_ref, out_ref):
    step = pl.program_id(0)
    first = jnp.where(step == 0, a_ref[...], b_ref[...])
    second = jnp.where(step == steps, c_ref[...], d_ref[...])

    @pl.when(step < steps)
    def _():
        rank = left_ref.shape[0] // 3
        high, middle, low = (left_ref[k * rank : (k + 1) * rank, :] for k in range(3))
        left = jnp.concatenate([high, middle, high, middle, low, high], axis=0)
        product = dot(left, right_ref[...], ((0,), (0,)))
        out_ref[...] = (one_ref[...] + dot(first, cot_ref[...], ((0,), (0,))) + product).astype(BF16)

    @pl.when(step >= steps)
    def _():
        out_ref[...] = (two_ref[...] + dot(second, cot_ref[...], ((0,), (0,)))).astype(BF16)


def finish(far, one, two, left3, right_wide, cot):
    depth, width = far[0].shape[0], one.shape[0]
    columns = cot.shape[1]
    steps = width // LAST
    low = lambda i: jnp.minimum(i, steps - 1)
    high = lambda i: jnp.maximum(i - steps, 0)
    return pl.pallas_call(
        lambda *refs: finish_kernel(steps, *refs),
        grid=(2 * steps,),
        in_specs=[
            *[pl.BlockSpec((depth, LAST), lambda i: (0, 0)) for _ in far],
            pl.BlockSpec((LAST, columns), lambda i: (low(i), 0)),
            pl.BlockSpec((LAST, columns), lambda i: (high(i), 0)),
            pl.BlockSpec((left3.shape[0], LAST), lambda i: (0, low(i))),
            pl.BlockSpec(right_wide.shape, lambda i: (0, 0)),
            pl.BlockSpec((depth, columns), lambda i: (0, 0)),
        ],
        out_specs=pl.BlockSpec((LAST, columns), lambda i: (i, 0)),
        out_shape=jax.ShapeDtypeStruct((2 * width, columns), BF16),
        compiler_params=pltpu.CompilerParams(vmem_limit_bytes=24 << 20),
        cost_estimate=pl.CostEstimate(
            flops=4 * depth * width * columns, bytes_accessed=4 * width * (depth + 3 * columns), transcendentals=0
        ),
    )(*far, one, two, left3, right_wide, cot)


def spread(x, axis):
    return jnp.broadcast_to(x, (lax.axis_size(axis),) + x.shape)


def shards(tokens, cotangent, error_buffer, start_basis):
    tokens, cot, error = tokens[0], cotangent[0], error_buffer[0]
    planes = lax.axis_size("tensor")
    replicas = lax.axis_size("dp")
    depth, d = tokens.shape
    columns, rank = start_basis.shape
    width = d // CHUNKS
    ring = Ring([tokens[:, c * width : (c + 1) * width] for c in range(CHUNKS)], "tensor")

    start3 = split_rows(start_basis.T)
    weights = join_rows(dot(start3, cot, ((1,), (1,))))
    weights = weights.reshape(rank, planes, depth).transpose(1, 0, 2)
    moved = [ring.step()]
    moved.append(ring.step(weights))
    weight = after(jnp.sum(lax.all_to_all(weights, "tensor", 0, 0), axis=0), *moved[0])
    moved.append(ring.step(weight))
    left_part = join_rows(dot(split_rows(weight), tokens, ((1,), (0,))) + dot(start3, error, ((1,), (1,))))
    height = d // replicas
    left_part = left_part.reshape(rank, replicas, height).transpose(1, 0, 2)
    left_rows = after(jnp.sum(lax.all_to_all(left_part, "dp", 0, 0), axis=0), *moved[1])
    left_rows = spread(left_rows, "tensor")
    moved.append(ring.step(left_rows))
    whole_rows = after(jnp.sum(lax.all_to_all(left_rows, "tensor", 0, 0), axis=0), *moved[2])
    moved.append(ring.step(whole_rows))
    half = planes // 2
    place = lax.axis_index("tensor") * depth
    turned = lax.dynamic_slice_in_dim(jnp.concatenate([cot, cot], axis=0), place, planes * depth, 0)
    early = jnp.concatenate([turned[: half * depth], turned[(half + 1) * depth :]], axis=0)
    cot_last = turned[half * depth : (half + 1) * depth]
    left = lax.all_to_all(spread(whole_rows, "dp"), "dp", 0, 0)
    left = after(left.transpose(1, 0, 2).reshape(rank, d), early, cot_last, *moved[3])

    left3 = split_rows(left)
    mine = lax.dynamic_slice_in_dim(left, lax.axis_index("dp") * height, height, 1)
    inner = spread(join_rows(dot(left3, tokens, ((1,), (1,)))), "tensor")
    moved.append(ring.step(inner))
    inverse = factor(after(left3, inner))
    inner = lax.all_to_all(inner, "tensor", 0, 0).transpose(1, 0, 2).reshape(rank, planes * depth)
    inner = after(inner, inverse, mine, *moved[4])
    right_part = join_rows(dot(split_rows(inner), cot, ((1,), (0,))) + dot(left3, error, ((1,), (0,))))
    right_part = spread(right_part, "dp")
    far = ring.last(right_part)
    blocks = ring.blocks
    one = early_partial(0, blocks[0][:half] + blocks[0][half + 1 :], early, error)
    parts = after(lax.all_to_all(right_part, "dp", 0, 0), one, *moved[5])
    decompressed, right_wide = solve(inverse, parts, mine)

    two = partial(width, blocks[1][:half] + blocks[1][half + 1 :], early, right_wide, left3, error)
    out = finish(far, one, two, left3, right_wide, cot_last)
    return decompressed, out[None]


def solution(mesh):
    in_specs = (
        P("dp", "tensor", None),
        P("dp", None, "tensor"),
        P("dp", None, "tensor"),
        P("tensor", None),
    )
    out_specs = (P("dp", "tensor"), P("dp", None, "tensor"))
    return jax.shard_map(shards, mesh=mesh, in_specs=in_specs, out_specs=out_specs, check_vma=False)
```
